32 devices in a mesh: shots: 2 (over x), blk: 16 (over z, y, core).
Axes of the slice: x: 2, y: 2, z: 4, core: 2. Of those that a mesh axis runs over, the one named last changes fastest.
Arguments:
- source_prev: float32 [32, 8, 64, 256], P(('shots', 'blk')), parts along dimension 0, may hold values from -8 to 8
- source_cur: float32 [32, 8, 64, 256], P(('shots', 'blk')), parts along dimension 0, may hold values from -8 to 8
- receiver_prev: float32 [32, 8, 64, 256], P(('shots', 'blk')), parts along dimension 0, may hold values from -8 to 8
- receiver_cur: float32 [32, 8, 64, 256], P(('shots', 'blk')), parts along dimension 0, may hold values from -8 to 8
- coef_horiz: float32 [16, 8, 64, 256], P('blk'), may hold values from 0.08 to 0.2
- coef_vert: float32 [16, 8, 64, 256], P('blk'), may hold values from 0.04 to 0.1
- coef_mixed: float32 [16, 8, 64, 256], P('blk'), may hold values from -0.05 to 0.05
- live_depth: int32 [16, 8, 64], P('blk'), may hold values from 1 to 256
- offsets: int32 [9], replicated, may hold values from 0 to 8, each once
- image_in: float32 [9, 32, 8, 64, 256], P(None, ('shots', 'blk')), parts along dimension 1, may hold values from -6 to 6
Outputs:
- image_out: float32 [9, 32, 8, 64, 256], P(None, ('shots', 'blk')), parts along dimension 1
- source_last: float32 [32, 8, 64, 256], P(('shots', 'blk')), parts along dimension 0
- receiver_last: float32 [32, 8, 64, 256], P(('shots', 'blk')), parts along dimension 0
The draws below stay inside these ranges and needn't reach their ends.
There are 2 independent parts, one for each index of `shots`. The reference program is written for one: setup_inputs(seed, part) draws one part's arguments, and reference() takes and returns one part's arrays. A program takes and returns all parts, laid end to end along the dimension named above; an argument that names none is the same for every part. Nothing has to cross between parts.
Inputs may be any that keep to these rules, and one draw needn't show every extreme that they name: offsets holds every value from 0 to 8 once.
All inputs are finite; a program needn't handle non-finite values.
Results may differ from the reference program's by a relative error of at most 0.0003.
Values sent between devices are 32-bit elements; how exact they have to be, the bound alone decides.
A program may use at most 64 MiB of HBM per device.

```python
import math
import jax
import jax.numpy as jnp
from jax import lax

BX = 8
NY = 64
NZ = 256
STEPS = 4
HMAX = 4
NOFF = 9
NBLK = 16


def wave_field(key, field_salt, rough_salt):
    shape = (NBLK, BX, NY, NZ)
    envelope_key = jax.random.fold_in(key, field_salt)
    phase_key, quarter_key = jax.random.split(envelope_key, 2)
    phases = jax.random.uniform(phase_key, (2,), jnp.float32, 0.0, 2.0 * math.pi)
    quarter = jax.random.randint(quarter_key, (), 0, 4).astype(jnp.float32)
    cell_x = lax.broadcasted_iota(jnp.float32, shape, 0) * BX + lax.broadcasted_iota(jnp.float32, shape, 1)
    cell_y = lax.broadcasted_iota(jnp.float32, shape, 2)
    cell_z = lax.broadcasted_iota(jnp.float32, shape, 3)
    envelope = 1.0 + 0.15 * jnp.sin(cell_x * (2.0 * math.pi / 37.0) + phases[0]) + 0.15 * jnp.sin(cell_y * (2.0 * math.pi / 29.0) + phases[1])
    pattern = jnp.cos(cell_z * (0.5 * math.pi) + 0.25 * math.pi + 0.5 * math.pi * quarter)
    rough_key = jax.random.fold_in(key, rough_salt)
    amplitude = 5.0
    rough = 0.8 * jax.random.truncated_normal(rough_key, -3.75, 3.75, shape, jnp.float32)
    return (amplitude * envelope * pattern + rough).astype(jnp.float32)


def draw_source_prev(key, part):
    return wave_field(key, 101, 1)


def draw_source_cur(key, part):
    return wave_field(key, 101, 2)


def draw_receiver_prev(key, part):
    return wave_field(key, 202, 3)


def draw_receiver_cur(key, part):
    return wave_field(key, 202, 4)


def touch_ends(array, rng, smallest, high):
    index_at = [jax.random.randint(jax.random.fold_in(rng, axis), (), 0, length) for axis, length in enumerate(array.shape)]
    widest = array.shape.index(max(array.shape))
    beside = index_at[:widest] + [(index_at[widest] + 1) % array.shape[widest]] + index_at[widest + 1:]
    return array.at[tuple(index_at)].set(smallest).at[tuple(beside)].set(high)


def shard_levels(rng, shape, cuts, smallest, largest):
    def one(dim, shards_of):
        draws = jax.random.uniform(jax.random.fold_in(jax.random.fold_in(rng, 6), dim), (shards_of,), jnp.float32, smallest / len(cuts), largest / len(cuts))
        return jnp.repeat(jnp.exp(draws), shape[dim] // shards_of).reshape((-1,) + (1,) * (len(shape) - dim - 1))

    factor_of = one(*cuts[0])
    for cut in cuts[1:]:
        factor_of = factor_of * one(*cut)
    return factor_of


def bell_draw(key, dims, scale, reach, cuts=(), kind=jnp.bfloat16):
    level = shard_levels(key, dims, cuts, -0.22, 0.18) if cuts else 1.0
    result = jax.random.normal(key, dims, jnp.float32) * scale * level
    return jnp.minimum(jnp.maximum(result, -reach), reach).astype(kind)


def setup_inputs(seed: int = 0, part: int = 0) -> dict:
    key_of = jax.random.split(jax.random.key(seed), 11)
    part_keys = jax.random.split(jax.random.fold_in(key_of[10], part), 11)
    return {
        "source_prev": draw_source_prev(jax.random.fold_in(jax.random.fold_in(key_of[10], part), 71), part),
        "source_cur": draw_source_cur(jax.random.fold_in(jax.random.fold_in(key_of[10], part), 71), part),
        "receiver_prev": draw_receiver_prev(jax.random.fold_in(jax.random.fold_in(key_of[10], part), 71), part),
        "receiver_cur": draw_receiver_cur(jax.random.fold_in(jax.random.fold_in(key_of[10], part), 71), part),
        "coef_horiz": jnp.clip(jnp.exp(math.log(0.2) - 0.91629077 * jax.random.uniform(key_of[4], (NBLK, BX, NY, NZ), jnp.float32) ** shard_levels(key_of[4], (NBLK, BX, NY, NZ), ((0, 16),), -0.2, 0.2)), 0.08, 0.2),
        "coef_vert": jnp.clip(jnp.exp(math.log(0.1) - 0.91629077 * jax.random.uniform(key_of[5], (NBLK, BX, NY, NZ), jnp.float32) ** shard_levels(key_of[5], (NBLK, BX, NY, NZ), ((0, 16),), -0.2, 0.2)), 0.04, 0.1),
        "coef_mixed": jnp.clip(jax.random.uniform(key_of[6], (NBLK, BX, NY, NZ), jnp.float32, -0.05, 0.05) * shard_levels(key_of[6], (NBLK, BX, NY, NZ), ((0, 16),), -0.4, 0.0), -0.05, 0.05),
        "live_depth": touch_ends(jax.random.randint(key_of[7], (NBLK, BX, NY), 1, NZ + 1), jax.random.fold_in(key_of[7], 1), 1, NZ).astype(jnp.int32),
        "offsets": jax.random.permutation(key_of[8], NOFF).astype(jnp.int32),
        "image_in": bell_draw(part_keys[9], (NOFF, NBLK, BX, NY, NZ), 1.0, 6.0, ((1, 16),), jnp.float32),
    }


second_w = (-205.0 / 72.0, 8.0 / 5.0, -1.0 / 5.0, 8.0 / 315.0, -1.0 / 560.0)
first_w = (4.0 / 5.0, -1.0 / 5.0, 4.0 / 105.0, -1.0 / 280.0)


def stencil(padded_xy, coef_horiz, coef_vert, coef_mixed):
    count_x = padded_xy.shape[0] - 8
    count_y = padded_xy.shape[1] - 8
    depth = padded_xy.shape[2]
    padded = jnp.pad(padded_xy, ((0, 0), (0, 0), (4, 4)))

    def take(a, b, c):
        return padded[4 + a:4 + a + count_x, 4 + b:4 + b + count_y, 4 + c:4 + c + depth]

    center = take(0, 0, 0)
    horiz = (2.0 * second_w[0]) * center
    vert = second_w[0] * center
    deriv_z = jnp.zeros((count_x + 8, count_y, depth), jnp.float32)
    for k in range(1, 5):
        horiz = horiz + second_w[k] * (take(k, 0, 0) + take(-k, 0, 0) + take(0, k, 0) + take(0, -k, 0))
        vert = vert + second_w[k] * (take(0, 0, k) + take(0, 0, -k))
        deriv_z = deriv_z + first_w[k - 1] * (padded[:, 4:4 + count_y, 4 + k:4 + k + depth] - padded[:, 4:4 + count_y, 4 - k:4 - k + depth])
    mixed = jnp.zeros((count_x, count_y, depth), jnp.float32)
    for k in range(1, 5):
        mixed = mixed + first_w[k - 1] * (deriv_z[4 + k:4 + k + count_x] - deriv_z[4 - k:4 - k + count_x])
    return coef_horiz * horiz + coef_vert * vert + coef_mixed * mixed


def image_terms(src_pad, rec_pad, width, offsets, mute):
    count = mute.shape[0]
    terms = []
    for slot in range(NOFF):
        shift = offsets[slot] - HMAX
        left = lax.dynamic_slice_in_dim(src_pad, (width - shift).astype(jnp.int32), count, 0)
        right = lax.dynamic_slice_in_dim(rec_pad, (width + shift).astype(jnp.int32), count, 0)
        terms.append(mute * left * right)
    return jnp.stack(terms)


def to_grid(blocks):
    return blocks.reshape((NBLK * BX,) + blocks.shape[2:])


def from_grid(grid):
    return grid.reshape((NBLK, BX) + grid.shape[1:])


def step_pad(field):
    return jnp.pad(field, ((4, 4), (4, 4), (0, 0)))


def reference(source_prev, source_cur, receiver_prev, receiver_cur, coef_horiz, coef_vert, coef_mixed, live_depth, offsets, image_in):
    source_prev = to_grid(source_prev)
    source_cur = to_grid(source_cur)
    receiver_prev = to_grid(receiver_prev)
    receiver_cur = to_grid(receiver_cur)
    coef_horiz = to_grid(coef_horiz)
    coef_vert = to_grid(coef_vert)
    coef_mixed = to_grid(coef_mixed)
    depth_grid = to_grid(live_depth)
    depth_ids = lax.broadcasted_iota(jnp.int32, source_cur.shape, 2)
    mute = (depth_ids < depth_grid[:, :, None]).astype(jnp.float32)
    image = jax.vmap(to_grid)(image_in)
    for step in range(STEPS):
        src_new = 2.0 * source_cur - source_prev + stencil(step_pad(source_cur), coef_horiz, coef_vert, coef_mixed)
        rec_new = 2.0 * receiver_cur - receiver_prev + stencil(step_pad(receiver_cur), coef_horiz, coef_vert, coef_mixed)
        source_prev, source_cur = source_cur, src_new
        receiver_prev, receiver_cur = receiver_cur, rec_new
        if (step + 1) % (STEPS // 2) == 0:
            src_pad = jnp.pad(source_cur, ((HMAX, HMAX), (0, 0), (0, 0)))
            rec_pad = jnp.pad(receiver_cur, ((HMAX, HMAX), (0, 0), (0, 0)))
            image = image + image_terms(src_pad, rec_pad, HMAX, offsets, mute)
    return jax.vmap(from_grid)(image), from_grid(source_cur), from_grid(receiver_cur)
```

```python
import functools

import jax
import jax.numpy as jnp
import ml_dtypes
import numpy as np
from jax import lax
from jax.experimental import pallas as pl
from jax.experimental.pallas import tpu as pltpu
from jax.sharding import PartitionSpec as P

STEPS = 4
RAD = 4
NOFF = 9
MESH = pl.DeviceIdType.MESH

second_w = (-205.0 / 72.0, 8.0 / 5.0, -1.0 / 5.0, 8.0 / 315.0, -1.0 / 560.0)
first_w = (4.0 / 5.0, -1.0 / 5.0, 4.0 / 105.0, -1.0 / 280.0)
SECOND_SCALE = 5040.0
FIRST_SCALE = 840.0
second_int = (0, 8064, -1008, 128, -9)
first_int = (672, -168, 32, -3)


def band(size, weights, odd):
    out = np.zeros((size, size), np.float32)
    for k, w in weights:
        out += w * np.eye(size, k=-k) + (-w if odd else w) * np.eye(size, k=k)
    return out


def depth_weights(nz):
    dzz = band(nz, [(k, second_int[k]) for k in range(1, 5)], False)
    dz = band(nz, [(k + 1, first_int[k]) for k in range(4)], True)
    return np.concatenate([dzz, dz], 1).astype(ml_dtypes.bfloat16)


def row_weights(ny, planes):
    dyy = band(ny, [(k, second_int[k]) for k in range(1, 5)], False)
    return np.kron(np.eye(planes), dyy).astype(ml_dtypes.bfloat16)


def split(value):
    high = value.astype(jnp.bfloat16)
    return high, (value - high.astype(jnp.float32)).astype(jnp.bfloat16)


def dot(a, b):
    return jnp.dot(a, b, preferred_element_type=jnp.float32)


def wave_kernel(
    count, sp, sc, rp, rc, ch_in, cv_in, cm_in, wz_in, wy_in, snaps,
    wave, dz, base, ch, cv, cm, wz, wy, load_sem, send_sem, recv_sem, out_sem, last_sem,
):
    bx, ny, nz = ch.shape
    rows = RAD * ny
    me = lax.axis_index("blk")
    outer = lax.rem(me, 2)
    inner = 1 - outer

    def beside(side):
        return me - 1 + 2 * side

    def there(side):
        return (beside(side) >= 0) & (beside(side) < count)

    loads = []
    for f, (prev, cur) in enumerate(((sp, sc), (rp, rc))):
        loads.append((prev.at[0], wave.at[0, f, pl.ds(RAD, bx)]))
        loads.append((cur.at[0], wave.at[1, f, pl.ds(RAD, bx)]))
    loads += [(ch_in.at[0], ch), (cv_in.at[0], cv), (cm_in.at[0], cm), (wz_in, wz), (wy_in, wy)]
    loads = [pltpu.make_async_copy(a, b, load_sem.at[j]) for j, (a, b) in enumerate(loads)]
    for load in loads:
        load.start()

    barrier = pltpu.get_barrier_semaphore()
    for side in (0, 1):
        @pl.when(there(side))
        def _():
            pl.semaphore_signal(
                barrier, inc=1, device_id={"blk": beside(side)}, device_id_type=MESH
            )
    peers = jnp.where(there(0), 1, 0) + jnp.where(there(1), 1, 0)
    pl.semaphore_wait(barrier, peers)

    def copy(level, f, way, to, src=None):
        if src is None:
            src = wave.at[level, f, pl.ds(RAD + (bx - RAD) * way, RAD)]
        return pltpu.make_async_remote_copy(
            src_ref=src,
            dst_ref=wave.at[level, f, pl.ds((RAD + bx) * (1 - way), RAD)],
            send_sem=send_sem.at[level, f, way],
            recv_sem=recv_sem.at[level, f, way],
            device_id={"blk": beside(to)},
            device_id_type=MESH,
        )

    def first_copy(f, way):
        return copy(1, f, way, way, (sc, rc)[f].at[0, pl.ds((bx - RAD) * way, RAD)])

    for way in (outer, inner):
        for f in (0, 1):
            @pl.when(there(way))
            def _():
                first_copy(f, way).start()

    for side in (0, 1):
        @pl.when(jnp.logical_not(there(side)))
        def _():
            def clear(level, carry):
                for f in (0, 1):
                    wave[level, f, pl.ds((RAD + bx) * side, RAD)] = jnp.zeros(
                        (RAD, ny, nz), jnp.float32
                    )
                return carry

            lax.fori_loop(1, STEPS + 2, clear, 0)

    def arrive(level, f, side):
        @pl.when(there(side))
        def _():
            copy(level, f, 1 - side, side).wait_recv()

    def local(level, f):
        def group(g, carry):
            own = pl.ds(RAD * g, RAD)
            at = pl.ds(RAD + RAD * g, RAD)
            now = wave[level, f, at]
            high, low = split(now.reshape(rows, nz))
            both = dot(high, wz[...]) + dot(low, wz[...])
            side = dot(wy[...], high) + dot(wy[...], low)
            dz[f, at] = both[:, nz:].reshape(RAD, ny, nz)
            dzz = both[:, :nz].reshape(RAD, ny, nz) * (1.0 / SECOND_SCALE) + second_w[0] * now
            dyy = side.reshape(RAD, ny, nz) * (1.0 / SECOND_SCALE) + 2.0 * second_w[0] * now
            base[f, own] = (
                2.0 * now - wave[level - 1, f, at] + ch[own] * dyy + cv[own] * dzz
            )
            return carry

        lax.fori_loop(0, bx // RAD, group, 0)

    def rim(level, f, side):
        at = pl.ds((RAD + bx) * side, RAD)
        high, low = split(wave[level, f, at].reshape(rows, nz))
        weights = wz[:, nz:]
        dz[f, at] = (dot(high, weights) + dot(low, weights)).reshape(RAD, ny, nz)

    def update(level, f, side):
        half = ny // 2

        def plane(j, carry):
            own = (bx - RAD) * side + j
            x = own + RAD
            for r in (0, half):
                at = pl.ds(r, half)
                flat, cross = None, None
                for k in range(1, RAD + 1):
                    a = second_w[k] * (wave[level, f, x + k, at] + wave[level, f, x - k, at])
                    b = (first_w[k - 1] / FIRST_SCALE) * (dz[f, x + k, at] - dz[f, x - k, at])
                    flat = a if flat is None else flat + a
                    cross = b if cross is None else cross + b
                wave[level + 1, f, x, at] = (
                    base[f, own, at] + ch[own, at] * flat + cm[own, at] * cross
                )
            return carry

        lax.fori_loop(0, RAD, plane, 0)

    for load in loads:
        load.wait()
    for f in (0, 1):
        local(1, f)

    mid = [pltpu.make_async_copy(wave.at[3, f], snaps.at[0, f], out_sem.at[f]) for f in (0, 1)]

    def step(level, carry):
        for f in (0, 1):
            for side in (outer, inner):
                arrive(level, f, side)
                rim(level, f, side)
                update(level, f, side)

                @pl.when(there(side))
                def _():
                    copy(level + 1, f, side, side).start()

            @pl.when(level < STEPS)
            def _():
                local(level + 1, f)

            @pl.when(level == 3)
            def _():
                mid[f].start()
        return carry

    lax.fori_loop(1, STEPS + 1, step, 0)

    last = STEPS + 1
    done = []
    for f in (0, 1):
        own = pl.ds(RAD, bx)
        done.append(
            pltpu.make_async_copy(wave.at[last, f, own], snaps.at[1, f, own], last_sem.at[f, 2])
        )
        done[-1].start()
    for f in (0, 1):
        for j, side in enumerate((inner, outer)):
            arrive(last, f, side)
            at = pl.ds((RAD + bx) * side, RAD)
            done.append(
                pltpu.make_async_copy(wave.at[last, f, at], snaps.at[1, f, at], last_sem.at[f, j])
            )
            done[-1].start()
    for item in mid + done:
        item.wait()
    for way in (0, 1):
        @pl.when(there(way))
        def _():
            for f in (0, 1):
                first_copy(f, way).wait_send()

            def sent(level, carry):
                for f in (0, 1):
                    copy(level, f, way, way).wait_send()
                return carry

            lax.fori_loop(2, STEPS + 2, sent, 0)


def image_kernel(offsets, live, snaps, image_in, image_out, source_last, receiver_last, mute):
    slot = pl.program_id(0)
    bx, ny, nz = mute.shape

    @pl.when(slot == 0)
    def _():
        row_ids = lax.broadcasted_iota(jnp.int32, (ny, ny), 0)
        diagonal = row_ids == lax.broadcasted_iota(jnp.int32, (ny, ny), 1)
        depth_ids = lax.broadcasted_iota(jnp.int32, (ny, nz), 1).astype(jnp.float32)
        for x in range(bx):
            depths = live[0, pl.ds(x, 1), :].astype(jnp.float32)
            column = jnp.sum(jnp.where(diagonal, depths, 0.0), axis=1, keepdims=True)
            mute[x] = (depth_ids < column).astype(jnp.float32)
        source_last[0] = snaps[1, 0, pl.ds(RAD, bx)]
        receiver_last[0] = snaps[1, 1, pl.ds(RAD, bx)]

    shift = offsets[slot] - RAD

    def plane(x, carry):
        left, right = RAD + x - shift, RAD + x + shift
        image_out[0, 0, x] = image_in[0, 0, x] + mute[x] * (
            snaps[0, 0, left] * snaps[0, 1, right] + snaps[1, 0, left] * snaps[1, 1, right]
        )
        return carry

    lax.fori_loop(0, bx, plane, 0)


def per_device(
    count,
    source_prev,
    source_cur,
    receiver_prev,
    receiver_cur,
    coef_horiz,
    coef_vert,
    coef_mixed,
    live_depth,
    offsets,
    image_in,
):
    _, bx, ny, nz = source_cur.shape
    f32 = jnp.float32
    slab = pltpu.VMEM((bx, ny, nz), f32)
    wz = jnp.asarray(depth_weights(nz))
    wy = jnp.asarray(row_weights(ny, RAD))
    full = bx + 2 * RAD
    any_space = pl.BlockSpec(memory_space=pl.ANY)
    snaps = pl.pallas_call(
        functools.partial(wave_kernel, count),
        out_shape=jax.ShapeDtypeStruct((2, 2, full, ny, nz), f32),
        in_specs=[any_space] * 9,
        out_specs=any_space,
        scratch_shapes=[
            pltpu.VMEM((STEPS + 2, 2, full, ny, nz), f32),
            pltpu.VMEM((2, full, ny, nz), f32),
            pltpu.VMEM((2, bx, ny, nz), f32),
            slab,
            slab,
            slab,
            pltpu.VMEM(wz.shape, jnp.bfloat16),
            pltpu.VMEM(wy.shape, jnp.bfloat16),
            pltpu.SemaphoreType.DMA((9,)),
            pltpu.SemaphoreType.DMA((STEPS + 2, 2, 2)),
            pltpu.SemaphoreType.DMA((STEPS + 2, 2, 2)),
            pltpu.SemaphoreType.DMA((2,)),
            pltpu.SemaphoreType.DMA((2, 3)),
        ],
        compiler_params=pltpu.CompilerParams(
            collective_id=0, has_side_effects=True, vmem_limit_bytes=40 * 2**20
        ),
        name="wave_steps",
    )(
        source_prev, source_cur, receiver_prev, receiver_cur,
        coef_horiz, coef_vert, coef_mixed, wz, wy,
    )
    slot_spec = pl.BlockSpec((1, 1, bx, ny, nz), lambda k, off: (k, 0, 0, 0, 0))
    last_spec = pl.BlockSpec((1, bx, ny, nz), lambda k, off: (0, 0, 0, 0))
    return pl.pallas_call(
        image_kernel,
        grid_spec=pltpu.PrefetchScalarGridSpec(
            num_scalar_prefetch=1,
            grid=(NOFF,),
            in_specs=[
                pl.BlockSpec((1, bx, ny), lambda k, off: (0, 0, 0)),
                pl.BlockSpec((2, 2, full, ny, nz), lambda k, off: (0, 0, 0, 0, 0)),
                slot_spec,
            ],
            out_specs=[slot_spec, last_spec, last_spec],
            scratch_shapes=[slab],
        ),
        out_shape=[
            jax.ShapeDtypeStruct(image_in.shape, f32),
            jax.ShapeDtypeStruct(source_cur.shape, f32),
            jax.ShapeDtypeStruct(receiver_cur.shape, f32),
        ],
        compiler_params=pltpu.CompilerParams(vmem_limit_bytes=40 * 2**20),
        name="image_terms",
    )(offsets, live_depth, snaps, image_in)


def solution(mesh):
    in_specs = (
        P(("shots", "blk"), None, None, None),
        P(("shots", "blk"), None, None, None),
        P(("shots", "blk"), None, None, None),
        P(("shots", "blk"), None, None, None),
        P("blk", None, None, None),
        P("blk", None, None, None),
        P("blk", None, None, None),
        P("blk", None, None),
        P(),
        P(None, ("shots", "blk"), None, None, None),
    )
    out_specs = (
        P(None, ("shots", "blk"), None, None, None),
        P(("shots", "blk"), None, None, None),
        P(("shots", "blk"), None, None, None),
    )
    return jax.shard_map(
        functools.partial(per_device, mesh.shape["blk"]),
        mesh=mesh,
        in_specs=in_specs,
        out_specs=out_specs,
        check_vma=False,
    )
```

```python
import functools

import jax
import jax.numpy as jnp
from jax import lax
from jax.experimental import pallas as pl
from jax.experimental.pallas import tpu as pltpu
from jax.sharding import PartitionSpec as P

STEPS = 4
RAD = 4
NOFF = 9
MESH = pl.DeviceIdType.MESH

second_w = (-205.0 / 72.0, 8.0 / 5.0, -1.0 / 5.0, 8.0 / 315.0, -1.0 / 560.0)
first_w = (4.0 / 5.0, -1.0 / 5.0, 4.0 / 105.0, -1.0 / 280.0)
SECOND_SCALE = 5040.0
FIRST_SCALE = 840.0
second_int = (0, 8064, -1008, 128, -9)
first_int = (672, -168, 32, -3)


def band(size, weights, odd, block):
    row = lax.broadcasted_iota(jnp.int32, (size, size), 0)
    col = lax.broadcasted_iota(jnp.int32, (size, size), 1)
    out = jnp.zeros((size, size), jnp.float32)
    for k, w in weights:
        out = jnp.where(row - col == k, float(w), out)
        out = jnp.where(col - row == k, float(-w if odd else w), out)
    for edge in range(block, size, block):
        out = jnp.where((row < edge) == (col < edge), out, 0.0)
    return out.astype(jnp.bfloat16)


def split(value):
    high = value.astype(jnp.bfloat16)
    return high, (value - high.astype(jnp.float32)).astype(jnp.bfloat16)


def dot(a, b):
    return jnp.dot(a, b, preferred_element_type=jnp.float32)


def wave_kernel(
    count, sp, sc, rp, rc, ch_in, cv_in, cm_in, image_in, live, offsets,
    snaps, image_mid, mute_out,
    wave, dz, base, ch, cv, cm, wz, wy, image, snap, mute,
    load_sem, send_sem, recv_sem, out_sem, last_sem,
):
    bx, ny, nz = ch.shape
    rows = RAD * ny
    me = lax.axis_index("blk")
    outer = lax.rem(me, 2)
    inner = 1 - outer

    def beside(side):
        return me - 1 + 2 * side

    def there(side):
        return (beside(side) >= 0) & (beside(side) < count)

    loads = []
    for f, (prev, cur) in enumerate(((sp, sc), (rp, rc))):
        loads.append((prev.at[0], wave.at[0, f, pl.ds(RAD, bx)]))
        loads.append((cur.at[0], wave.at[1, f, pl.ds(RAD, bx)]))
    loads += [(ch_in.at[0], ch), (cv_in.at[0], cv), (cm_in.at[0], cm)]
    loads = [pltpu.make_async_copy(a, b, load_sem.at[j]) for j, (a, b) in enumerate(loads)]
    for load in loads:
        load.start()

    barrier = pltpu.get_barrier_semaphore()
    for side in (0, 1):
        @pl.when(there(side))
        def _():
            pl.semaphore_signal(
                barrier, inc=1, device_id={"blk": beside(side)}, device_id_type=MESH
            )
    peers = jnp.where(there(0), 1, 0) + jnp.where(there(1), 1, 0)
    pl.semaphore_wait(barrier, peers)

    def copy(level, f, way, to, src=None):
        if src is None:
            src = wave.at[level, f, pl.ds(RAD + (bx - RAD) * way, RAD)]
        return pltpu.make_async_remote_copy(
            src_ref=src,
            dst_ref=wave.at[level, f, pl.ds((RAD + bx) * (1 - way), RAD)],
            send_sem=send_sem.at[level, f, way],
            recv_sem=recv_sem.at[level, f, way],
            device_id={"blk": beside(to)},
            device_id_type=MESH,
        )

    def first_copy(f, way):
        return copy(1, f, way, way, (sc, rc)[f].at[0, pl.ds((bx - RAD) * way, RAD)])

    for f, way in ((0, outer), (0, inner), (1, inner)):
        @pl.when(there(way))
        def _():
            first_copy(f, way).start()

    image_load = pltpu.make_async_copy(image_in.at[:, 0], image, out_sem.at[2])
    image_load.start()

    for side in (0, 1):
        @pl.when(jnp.logical_not(there(side)))
        def _():
            def clear(level, carry):
                for f in (0, 1):
                    wave[level, f, pl.ds((RAD + bx) * side, RAD)] = jnp.zeros(
                        (RAD, ny, nz), jnp.float32
                    )
                return carry

            lax.fori_loop(1, STEPS + 2, clear, 0)

    def arrive(level, f, side):
        @pl.when(there(side))
        def _():
            copy(level, f, 1 - side, side).wait_recv()

    def local(level, f):
        def group(g, carry):
            own = pl.ds(RAD * g, RAD)
            at = pl.ds(RAD + RAD * g, RAD)
            now = wave[level, f, at]
            high, low = split(now.reshape(rows, nz))
            both = dot(high, wz[...]) + dot(low, wz[...])
            side = dot(wy[...], high) + dot(wy[...], low)
            dz[f, at] = both[:, nz:].reshape(RAD, ny, nz)
            dzz = both[:, :nz].reshape(RAD, ny, nz) * (1.0 / SECOND_SCALE) + second_w[0] * now
            dyy = side.reshape(RAD, ny, nz) * (1.0 / SECOND_SCALE) + 2.0 * second_w[0] * now
            base[f, own] = (
                2.0 * now - wave[level - 1, f, at] + ch[own] * dyy + cv[own] * dzz
            )
            return carry

        lax.fori_loop(0, bx // RAD, group, 0)

    def rim(level, f, side):
        at = pl.ds((RAD + bx) * side, RAD)
        high, low = split(wave[level, f, at].reshape(rows, nz))
        weights = wz[:, nz:]
        dz[f, at] = (dot(high, weights) + dot(low, weights)).reshape(RAD, ny, nz)

    def update(level, f, side):
        half = ny // 2

        def plane(j, carry):
            own = (bx - RAD) * side + j
            x = own + RAD
            for r in (0, half):
                at = pl.ds(r, half)
                flat, cross = None, None
                for k in range(1, RAD + 1):
                    a = second_w[k] * (wave[level, f, x + k, at] + wave[level, f, x - k, at])
                    b = (first_w[k - 1] / FIRST_SCALE) * (dz[f, x + k, at] - dz[f, x - k, at])
                    flat = a if flat is None else flat + a
                    cross = b if cross is None else cross + b
                wave[level + 1, f, x, at] = (
                    base[f, own, at] + ch[own, at] * flat + cm[own, at] * cross
                )
            return carry

        lax.fori_loop(0, RAD, plane, 0)

    seconds = [(k, second_int[k]) for k in range(1, RAD + 1)]
    firsts = [(k + 1, first_int[k]) for k in range(RAD)]
    wz[:, :nz] = band(nz, seconds, False, nz)
    wz[:, nz:] = band(nz, firsts, True, nz)
    wy[...] = band(rows, seconds, False, ny)
    for load in loads:
        load.wait()
    for f in (0, 1):
        local(1, f)

    @pl.when(there(outer))
    def _():
        first_copy(0, outer).wait_send()
        first_copy(1, outer).start()

    mid = [pltpu.make_async_copy(wave.at[3, f], snap.at[f], out_sem.at[f]) for f in (0, 1)]

    def step(level, carry):
        for f in (0, 1):
            for side in (outer, inner):
                arrive(level, f, side)
                rim(level, f, side)
                update(level, f, side)

                @pl.when(there(side))
                def _():
                    copy(level + 1, f, side, side).start()

            @pl.when(level < STEPS)
            def _():
                local(level + 1, f)

            @pl.when(level == 3)
            def _():
                mid[f].start()
        return carry

    lax.fori_loop(1, STEPS + 1, step, 0)

    last = STEPS + 1
    done = []
    for f in (0, 1):
        own = pl.ds(RAD, bx)
        done.append(
            pltpu.make_async_copy(wave.at[last, f, own], snaps.at[f, own], last_sem.at[f, 2])
        )
        done[-1].start()

    row_ids = lax.broadcasted_iota(jnp.int32, (ny, ny), 0)
    diagonal = row_ids == lax.broadcasted_iota(jnp.int32, (ny, ny), 1)
    depth_ids = lax.broadcasted_iota(jnp.int32, (ny, nz), 1).astype(jnp.float32)
    for x in range(bx):
        depths = live[0, pl.ds(x, 1), :].astype(jnp.float32)
        column = jnp.sum(jnp.where(diagonal, depths, 0.0), axis=1, keepdims=True)
        mute[x] = (depth_ids < column).astype(jnp.float32)
    done.append(pltpu.make_async_copy(mute, mute_out, out_sem.at[3]))
    done[-1].start()
    for item in mid + [image_load]:
        item.wait()

    def slot_terms(slot, carry):
        shift = offsets[slot] - RAD

        def plane(x, inside):
            image[slot, x] += mute[x] * snap[0, RAD + x - shift] * snap[1, RAD + x + shift]
            return inside

        return lax.fori_loop(0, bx, plane, carry)

    lax.fori_loop(0, NOFF, slot_terms, 0)
    done.append(pltpu.make_async_copy(image, image_mid, out_sem.at[2]))
    done[-1].start()

    for f in (0, 1):
        for j, side in enumerate((inner, outer)):
            arrive(last, f, side)
            at = pl.ds((RAD + bx) * side, RAD)
            done.append(
                pltpu.make_async_copy(wave.at[last, f, at], snaps.at[f, at], last_sem.at[f, j])
            )
            done[-1].start()
    for item in done:
        item.wait()
    for way in (0, 1):
        @pl.when(there(way))
        def _():
            @pl.when(way == inner)
            def _():
                first_copy(0, way).wait_send()

            first_copy(1, way).wait_send()

            def sent(level, carry):
                for f in (0, 1):
                    copy(level, f, way, way).wait_send()
                return carry

            lax.fori_loop(2, STEPS + 2, sent, 0)


def image_kernel(offsets, snaps, mute, image_in, image_out, source_last, receiver_last, sems):
    slot = pl.program_id(0)
    bx = mute.shape[0]
    copies = [
        pltpu.make_async_copy(snaps.at[f, pl.ds(RAD, bx)], last.at[0], sems.at[f])
        for f, last in enumerate((source_last, receiver_last))
    ]

    @pl.when(slot == 0)
    def _():
        for item in copies:
            item.start()

    shift = offsets[slot] - RAD

    def plane(x, carry):
        image_out[0, 0, x] = image_in[0, x] + mute[x] * (
            snaps[0, RAD + x - shift] * snaps[1, RAD + x + shift]
        )
        return carry

    lax.fori_loop(0, bx, plane, 0)

    @pl.when(slot == pl.num_programs(0) - 1)
    def _():
        for item in copies:
            item.wait()


def per_device(
    count,
    source_prev,
    source_cur,
    receiver_prev,
    receiver_cur,
    coef_horiz,
    coef_vert,
    coef_mixed,
    live_depth,
    offsets,
    image_in,
):
    _, bx, ny, nz = source_cur.shape
    f32 = jnp.float32
    slab = pltpu.VMEM((bx, ny, nz), f32)
    full = bx + 2 * RAD
    hbm = pl.BlockSpec(memory_space=pltpu.HBM)
    any_space = pl.BlockSpec(memory_space=pl.ANY)
    snaps, image_mid, mute = pl.pallas_call(
        functools.partial(wave_kernel, count),
        out_shape=[
            jax.ShapeDtypeStruct((2, full, ny, nz), f32),
            jax.ShapeDtypeStruct((NOFF, bx, ny, nz), f32),
            jax.ShapeDtypeStruct((bx, ny, nz), f32),
        ],
        in_specs=[hbm] * 8
        + [pl.BlockSpec(memory_space=pltpu.VMEM), pl.BlockSpec(memory_space=pltpu.SMEM)],
        out_specs=[any_space] * 3,
        scratch_shapes=[
            pltpu.VMEM((STEPS + 2, 2, full, ny, nz), f32),
            pltpu.VMEM((2, full, ny, nz), f32),
            pltpu.VMEM((2, bx, ny, nz), f32),
            slab,
            slab,
            slab,
            pltpu.VMEM((nz, 2 * nz), jnp.bfloat16),
            pltpu.VMEM((RAD * ny, RAD * ny), jnp.bfloat16),
            pltpu.VMEM((NOFF, bx, ny, nz), f32),
            pltpu.VMEM((2, full, ny, nz), f32),
            slab,
            pltpu.SemaphoreType.DMA((7,)),
            pltpu.SemaphoreType.DMA((STEPS + 2, 2, 2)),
            pltpu.SemaphoreType.DMA((STEPS + 2, 2, 2)),
            pltpu.SemaphoreType.DMA((4,)),
            pltpu.SemaphoreType.DMA((2, 3)),
        ],
        compiler_params=pltpu.CompilerParams(
            collective_id=0, has_side_effects=True, vmem_limit_bytes=58 * 2**20
        ),
        name="wave_steps",
    )(
        source_prev, source_cur, receiver_prev, receiver_cur,
        coef_horiz, coef_vert, coef_mixed, image_in, live_depth, offsets,
    )
    slot_spec = pl.BlockSpec((1, 1, bx, ny, nz), lambda k, off: (k, 0, 0, 0, 0))
    return pl.pallas_call(
        image_kernel,
        grid_spec=pltpu.PrefetchScalarGridSpec(
            num_scalar_prefetch=1,
            grid=(NOFF,),
            in_specs=[
                pl.BlockSpec((2, full, ny, nz), lambda k, off: (0, 0, 0, 0)),
                pl.BlockSpec((bx, ny, nz), lambda k, off: (0, 0, 0)),
                pl.BlockSpec((1, bx, ny, nz), lambda k, off: (k, 0, 0, 0)),
            ],
            out_specs=[slot_spec, any_space, any_space],
            scratch_shapes=[pltpu.SemaphoreType.DMA((2,))],
        ),
        out_shape=[
            jax.ShapeDtypeStruct(image_in.shape, f32),
            jax.ShapeDtypeStruct(source_cur.shape, f32),
            jax.ShapeDtypeStruct(receiver_cur.shape, f32),
        ],
        compiler_params=pltpu.CompilerParams(vmem_limit_bytes=58 * 2**20),
        name="image_terms",
    )(offsets, snaps, mute, image_mid)


def solution(mesh):
    in_specs = (
        P(("shots", "blk"), None, None, None),
        P(("shots", "blk"), None, None, None),
        P(("shots", "blk"), None, None, None),
        P(("shots", "blk"), None, None, None),
        P("blk", None, None, None),
        P("blk", None, None, None),
        P("blk", None, None, None),
        P("blk", None, None),
        P(),
        P(None, ("shots", "blk"), None, None, None),
    )
    out_specs = (
        P(None, ("shots", "blk"), None, None, None),
        P(("shots", "blk"), None, None, None),
        P(("shots", "blk"), None, None, None),
    )
    return jax.shard_map(
        functools.partial(per_device, mesh.shape["blk"]),
        mesh=mesh,
        in_specs=in_specs,
        out_specs=out_specs,
        check_vma=False,
    )
```

```python
import functools

import jax
import jax.numpy as jnp
from jax import lax
from jax.experimental import pallas as pl
from jax.experimental.pallas import tpu as pltpu
from jax.sharding import PartitionSpec as P

STEPS = 4
RAD = 4
NOFF = 9
MESH = pl.DeviceIdType.MESH

second_w = (-205.0 / 72.0, 8.0 / 5.0, -1.0 / 5.0, 8.0 / 315.0, -1.0 / 560.0)
first_w = (4.0 / 5.0, -1.0 / 5.0, 4.0 / 105.0, -1.0 / 280.0)
SECOND_SCALE = 5040.0
FIRST_SCALE = 840.0
second_int = (0, 8064, -1008, 128, -9)
first_int = (672, -168, 32, -3)


def band(size, weights, odd, block):
    row = lax.broadcasted_iota(jnp.int32, (size, size), 0)
    col = lax.broadcasted_iota(jnp.int32, (size, size), 1)
    out = jnp.zeros((size, size), jnp.float32)
    for k, w in weights:
        out = jnp.where(row - col == k, float(w), out)
        out = jnp.where(col - row == k, float(-w if odd else w), out)
    for edge in range(block, size, block):
        out = jnp.where((row < edge) == (col < edge), out, 0.0)
    return out.astype(jnp.bfloat16)


def split(value):
    high = value.astype(jnp.bfloat16)
    return high, (value - high.astype(jnp.float32)).astype(jnp.bfloat16)


def dot(a, b):
    return jnp.dot(a, b, preferred_element_type=jnp.float32)


def wave_kernel(
    count, sp, sc, rp, rc, ch_in, cv_in, cm_in, image_in, live, offsets,
    snaps, image_mid, mute_out,
    wave, dz, base, ch, cv, cm, wz, wy, image, snap, mute,
    load_sem, send_sem, recv_sem, out_sem, last_sem,
):
    bx, ny, nz = ch.shape
    rows = RAD * ny
    me = lax.axis_index("blk")
    outer = lax.rem(me, 2)
    inner = 1 - outer

    def beside(side):
        return me - 1 + 2 * side

    def there(side):
        return (beside(side) >= 0) & (beside(side) < count)

    loads = []
    for f, (prev, cur) in enumerate(((sp, sc), (rp, rc))):
        loads.append((prev.at[0], wave.at[0, f, pl.ds(RAD, bx)]))
        loads.append((cur.at[0], wave.at[1, f, pl.ds(RAD, bx)]))
    loads += [(ch_in.at[0], ch), (cv_in.at[0], cv), (cm_in.at[0], cm)]
    loads = [pltpu.make_async_copy(a, b, load_sem.at[j]) for j, (a, b) in enumerate(loads)]
    for load in loads:
        load.start()

    barrier = pltpu.get_barrier_semaphore()
    for side in (0, 1):
        @pl.when(there(side))
        def _():
            pl.semaphore_signal(
                barrier, inc=1, device_id={"blk": beside(side)}, device_id_type=MESH
            )
    peers = jnp.where(there(0), 1, 0) + jnp.where(there(1), 1, 0)
    pl.semaphore_wait(barrier, peers)

    def copy(level, f, way, to, src=None):
        if src is None:
            src = wave.at[level, f, pl.ds(RAD + (bx - RAD) * way, RAD)]
        return pltpu.make_async_remote_copy(
            src_ref=src,
            dst_ref=wave.at[level, f, pl.ds((RAD + bx) * (1 - way), RAD)],
            send_sem=send_sem.at[level, f, way],
            recv_sem=recv_sem.at[level, f, way],
            device_id={"blk": beside(to)},
            device_id_type=MESH,
        )

    def first_copy(f, way):
        return copy(1, f, way, way, (sc, rc)[f].at[0, pl.ds((bx - RAD) * way, RAD)])

    for f, way in ((0, outer), (1, outer), (0, inner), (1, inner)):
        @pl.when(there(way))
        def _():
            first_copy(f, way).start()

    image_load = pltpu.make_async_copy(image_in.at[:, 0], image, out_sem.at[2])
    image_load.start()

    for side in (0, 1):
        @pl.when(jnp.logical_not(there(side)))
        def _():
            def clear(level, carry):
                for f in (0, 1):
                    wave[level, f, pl.ds((RAD + bx) * side, RAD)] = jnp.zeros(
                        (RAD, ny, nz), jnp.float32
                    )
                return carry

            lax.fori_loop(1, STEPS + 2, clear, 0)

    def arrive(level, f, side):
        @pl.when(there(side))
        def _():
            copy(level, f, 1 - side, side).wait_recv()

    def local(level, f):
        def group(g, carry):
            own = pl.ds(RAD * g, RAD)
            at = pl.ds(RAD + RAD * g, RAD)
            now = wave[level, f, at]
            high, low = split(now.reshape(rows, nz))
            both = dot(high, wz[...]) + dot(low, wz[...])
            side = dot(wy[...], high) + dot(wy[...], low)
            dz[f, at] = both[:, nz:].reshape(RAD, ny, nz)
            dzz = both[:, :nz].reshape(RAD, ny, nz) * (1.0 / SECOND_SCALE) + second_w[0] * now
            dyy = side.reshape(RAD, ny, nz) * (1.0 / SECOND_SCALE) + 2.0 * second_w[0] * now
            base[f, own] = (
                2.0 * now - wave[level - 1, f, at] + ch[own] * dyy + cv[own] * dzz
            )
            return carry

        lax.fori_loop(0, bx // RAD, group, 0)

    def rim(level, f, side):
        at = pl.ds((RAD + bx) * side, RAD)
        high, low = split(wave[level, f, at].reshape(rows, nz))
        weights = wz[:, nz:]
        dz[f, at] = (dot(high, weights) + dot(low, weights)).reshape(RAD, ny, nz)

    def update(level, f, side):
        half = ny // 2

        def plane(j, carry):
            own = (bx - RAD) * side + j
            x = own + RAD
            for r in (0, half):
                at = pl.ds(r, half)
                flat, cross = None, None
                for k in range(1, RAD + 1):
                    a = second_w[k] * (wave[level, f, x + k, at] + wave[level, f, x - k, at])
                    b = (first_w[k - 1] / FIRST_SCALE) * (dz[f, x + k, at] - dz[f, x - k, at])
                    flat = a if flat is None else flat + a
                    cross = b if cross is None else cross + b
                wave[level + 1, f, x, at] = (
                    base[f, own, at] + ch[own, at] * flat + cm[own, at] * cross
                )
            return carry

        lax.fori_loop(0, RAD, plane, 0)

    seconds = [(k, second_int[k]) for k in range(1, RAD + 1)]
    firsts = [(k + 1, first_int[k]) for k in range(RAD)]
    wz[:, :nz] = band(nz, seconds, False, nz)
    wz[:, nz:] = band(nz, firsts, True, nz)
    wy[...] = band(rows, seconds, False, ny)
    for load in loads:
        load.wait()
    for f in (0, 1):
        local(1, f)

    row_ids = lax.broadcasted_iota(jnp.int32, (ny, ny), 0)
    diagonal = row_ids == lax.broadcasted_iota(jnp.int32, (ny, ny), 1)
    depth_ids = lax.broadcasted_iota(jnp.int32, (ny, nz), 1).astype(jnp.float32)
    for x in range(bx):
        depths = live[0, pl.ds(x, 1), :].astype(jnp.float32)
        column = jnp.sum(jnp.where(diagonal, depths, 0.0), axis=1, keepdims=True)
        mute[x] = (depth_ids < column).astype(jnp.float32)
    mute_store = pltpu.make_async_copy(mute, mute_out, out_sem.at[3])
    mute_store.start()
    image_store = pltpu.make_async_copy(image, image_mid, out_sem.at[2])

    mid = [pltpu.make_async_copy(wave.at[3, f], snap.at[f], out_sem.at[f]) for f in (0, 1)]

    def slot_terms(slot, carry):
        shift = offsets[slot] - RAD

        def plane(x, inside):
            image[slot, x] += mute[x] * snap[0, RAD + x - shift] * snap[1, RAD + x + shift]
            return inside

        return lax.fori_loop(0, bx, plane, carry)

    def step(level, carry):
        for f in (0, 1):
            for side in (outer, inner):
                arrive(level, f, side)
                rim(level, f, side)
                update(level, f, side)

                @pl.when(there(side))
                def _():
                    copy(level + 1, f, side, side).start()

            @pl.when(level < STEPS)
            def _():
                local(level + 1, f)

            @pl.when(level == 3)
            def _():
                mid[f].start()
                if f == 1:
                    for item in mid + [image_load]:
                        item.wait()
                    lax.fori_loop(0, NOFF // 2, slot_terms, 0)

            if f == 0:
                @pl.when(level == STEPS)
                def _():
                    lax.fori_loop(NOFF // 2, NOFF, slot_terms, 0)
                    image_store.start()
        return carry

    lax.fori_loop(1, STEPS + 1, step, 0)

    last = STEPS + 1
    done = [mute_store, image_store]
    for f in (0, 1):
        own = pl.ds(RAD, bx)
        done.append(
            pltpu.make_async_copy(wave.at[last, f, own], snaps.at[f, own], last_sem.at[f, 2])
        )
        done[-1].start()

    for f in (0, 1):
        for j, side in enumerate((inner, outer)):
            arrive(last, f, side)
            at = pl.ds((RAD + bx) * side, RAD)
            done.append(
                pltpu.make_async_copy(wave.at[last, f, at], snaps.at[f, at], last_sem.at[f, j])
            )
            done[-1].start()
    for item in done:
        item.wait()
    for way in (0, 1):
        @pl.when(there(way))
        def _():
            for f in (0, 1):
                first_copy(f, way).wait_send()

            def sent(level, carry):
                for f in (0, 1):
                    copy(level, f, way, way).wait_send()
                return carry

            lax.fori_loop(2, STEPS + 2, sent, 0)


def image_kernel(
    offsets, snaps_in, mute_in, image_in, image_out, source_last, receiver_last,
    snaps, mute, image, load_sem, store_sem, side_sem,
):
    bx = mute.shape[0]
    sides = [
        pltpu.make_async_copy(snaps_in.at[0], snaps.at[0], side_sem.at[0]),
        pltpu.make_async_copy(snaps_in.at[1], snaps.at[1], side_sem.at[1]),
        pltpu.make_async_copy(mute_in, mute, side_sem.at[2]),
    ]
    for item in sides:
        item.start()

    def load(slot):
        return pltpu.make_async_copy(image_in.at[slot], image.at[slot], load_sem.at[slot])

    def store(slot):
        return pltpu.make_async_copy(image.at[slot], image_out.at[slot, 0], store_sem.at[slot])

    for slot in range(NOFF):
        load(slot).start()
    for item in sides:
        item.wait()
    lasts = [
        pltpu.make_async_copy(snaps.at[f, pl.ds(RAD, bx)], last.at[0], side_sem.at[3 + f])
        for f, last in enumerate((source_last, receiver_last))
    ]

    def terms(slot, carry):
        load(slot).wait()
        shift = offsets[slot] - RAD

        def plane(x, inside):
            image[slot, x] += mute[x] * snaps[0, RAD + x - shift] * snaps[1, RAD + x + shift]
            return inside

        lax.fori_loop(0, bx, plane, 0)
        store(slot).start()
        return carry

    lax.fori_loop(0, NOFF, terms, 0)
    for item in lasts:
        item.start()
    for slot in range(NOFF):
        store(slot).wait()
    for item in lasts:
        item.wait()


def per_device(
    count,
    source_prev,
    source_cur,
    receiver_prev,
    receiver_cur,
    coef_horiz,
    coef_vert,
    coef_mixed,
    live_depth,
    offsets,
    image_in,
):
    _, bx, ny, nz = source_cur.shape
    f32 = jnp.float32
    slab = pltpu.VMEM((bx, ny, nz), f32)
    full = bx + 2 * RAD
    hbm = pl.BlockSpec(memory_space=pltpu.HBM)
    any_space = pl.BlockSpec(memory_space=pl.ANY)
    snaps, image_mid, mute = pl.pallas_call(
        functools.partial(wave_kernel, count),
        out_shape=[
            jax.ShapeDtypeStruct((2, full, ny, nz), f32),
            jax.ShapeDtypeStruct((NOFF, bx, ny, nz), f32),
            jax.ShapeDtypeStruct((bx, ny, nz), f32),
        ],
        in_specs=[hbm] * 8
        + [pl.BlockSpec(memory_space=pltpu.VMEM), pl.BlockSpec(memory_space=pltpu.SMEM)],
        out_specs=[any_space] * 3,
        scratch_shapes=[
            pltpu.VMEM((STEPS + 2, 2, full, ny, nz), f32),
            pltpu.VMEM((2, full, ny, nz), f32),
            pltpu.VMEM((2, bx, ny, nz), f32),
            slab,
            slab,
            slab,
            pltpu.VMEM((nz, 2 * nz), jnp.bfloat16),
            pltpu.VMEM((RAD * ny, RAD * ny), jnp.bfloat16),
            pltpu.VMEM((NOFF, bx, ny, nz), f32),
            pltpu.VMEM((2, full, ny, nz), f32),
            slab,
            pltpu.SemaphoreType.DMA((7,)),
            pltpu.SemaphoreType.DMA((STEPS + 2, 2, 2)),
            pltpu.SemaphoreType.DMA((STEPS + 2, 2, 2)),
            pltpu.SemaphoreType.DMA((4,)),
            pltpu.SemaphoreType.DMA((2, 3)),
        ],
        compiler_params=pltpu.CompilerParams(
            collective_id=0, has_side_effects=True, vmem_limit_bytes=58 * 2**20
        ),
        name="wave_steps",
    )(
        source_prev, source_cur, receiver_prev, receiver_cur,
        coef_horiz, coef_vert, coef_mixed, image_in, live_depth, offsets,
    )
    return pl.pallas_call(
        image_kernel,
        in_specs=[pl.BlockSpec(memory_space=pltpu.SMEM)] + [hbm] * 3,
        out_specs=[hbm] * 3,
        scratch_shapes=[
            pltpu.VMEM((2, full, ny, nz), f32),
            slab,
            pltpu.VMEM((NOFF, bx, ny, nz), f32),
            pltpu.SemaphoreType.DMA((NOFF,)),
            pltpu.SemaphoreType.DMA((NOFF,)),
            pltpu.SemaphoreType.DMA((5,)),
        ],
        out_shape=[
            jax.ShapeDtypeStruct(image_in.shape, f32),
            jax.ShapeDtypeStruct(source_cur.shape, f32),
            jax.ShapeDtypeStruct(receiver_cur.shape, f32),
        ],
        compiler_params=pltpu.CompilerParams(vmem_limit_bytes=58 * 2**20),
        name="image_terms",
    )(offsets, snaps, mute, image_mid)


def solution(mesh):
    in_specs = (
        P(("shots", "blk"), None, None, None),
        P(("shots", "blk"), None, None, None),
        P(("shots", "blk"), None, None, None),
        P(("shots", "blk"), None, None, None),
        P("blk", None, None, None),
        P("blk", None, None, None),
        P("blk", None, None, None),
        P("blk", None, None),
        P(),
        P(None, ("shots", "blk"), None, None, None),
    )
    out_specs = (
        P(None, ("shots", "blk"), None, None, None),
        P(("shots", "blk"), None, None, None),
        P(("shots", "blk"), None, None, None),
    )
    return jax.shard_map(
        functools.partial(per_device, mesh.shape["blk"]),
        mesh=mesh,
        in_specs=in_specs,
        out_specs=out_specs,
        check_vma=False,
    )
```

```python
import functools

import jax
import jax.numpy as jnp
from jax import lax
from jax.experimental import pallas as pl
from jax.experimental.pallas import tpu as pltpu
from jax.sharding import PartitionSpec as P

STEPS = 4
RAD = 4
NOFF = 9
MESH = pl.DeviceIdType.MESH

second_w = (-205.0 / 72.0, 8.0 / 5.0, -1.0 / 5.0, 8.0 / 315.0, -1.0 / 560.0)
first_w = (4.0 / 5.0, -1.0 / 5.0, 4.0 / 105.0, -1.0 / 280.0)
SECOND_SCALE = 5040.0
FIRST_SCALE = 840.0
second_int = (0, 8064, -1008, 128, -9)
first_int = (672, -168, 32, -3)


def band(size, weights, odd, block):
    row = lax.broadcasted_iota(jnp.int32, (size, size), 0)
    col = lax.broadcasted_iota(jnp.int32, (size, size), 1)
    out = jnp.zeros((size, size), jnp.float32)
    for k, w in weights:
        out = jnp.where(row - col == k, float(w), out)
        out = jnp.where(col - row == k, float(-w if odd else w), out)
    for edge in range(block, size, block):
        out = jnp.where((row < edge) == (col < edge), out, 0.0)
    return out.astype(jnp.bfloat16)


def split(value):
    high = value.astype(jnp.bfloat16)
    return high, (value - high.astype(jnp.float32)).astype(jnp.bfloat16)


def dot(a, b):
    return jnp.dot(a, b, preferred_element_type=jnp.float32)


def wave_kernel(
    count, sp, sc, rp, rc, ch_in, cv_in, cm_in, image_in, live, offsets,
    snaps, image_mid, mute_out,
    wave, dz, base, ch, cv, cm, wz, wy, image, snap, mute,
    load_sem, send_sem, recv_sem, out_sem, last_sem,
):
    bx, ny, nz = ch.shape
    rows = RAD * ny
    me = lax.axis_index("blk")
    outer = lax.rem(me, 2)
    inner = 1 - outer

    def beside(side):
        return me - 1 + 2 * side

    def there(side):
        return (beside(side) >= 0) & (beside(side) < count)

    loads = []
    for f, (prev, cur) in enumerate(((sp, sc), (rp, rc))):
        loads.append((prev.at[0], wave.at[0, f, pl.ds(RAD, bx)]))
        loads.append((cur.at[0], wave.at[1, f, pl.ds(RAD, bx)]))
    loads += [(ch_in.at[0], ch), (cv_in.at[0], cv), (cm_in.at[0], cm)]
    loads = [pltpu.make_async_copy(a, b, load_sem.at[j]) for j, (a, b) in enumerate(loads)]
    for load in loads:
        load.start()

    barrier = pltpu.get_barrier_semaphore()
    for side in (0, 1):
        @pl.when(there(side))
        def _():
            pl.semaphore_signal(
                barrier, inc=1, device_id={"blk": beside(side)}, device_id_type=MESH
            )
    peers = jnp.where(there(0), 1, 0) + jnp.where(there(1), 1, 0)
    pl.semaphore_wait(barrier, peers)

    def copy(level, f, way, to, src=None):
        if src is None:
            src = wave.at[level, f, pl.ds(RAD + (bx - RAD) * way, RAD)]
        return pltpu.make_async_remote_copy(
            src_ref=src,
            dst_ref=wave.at[level, f, pl.ds((RAD + bx) * (1 - way), RAD)],
            send_sem=send_sem.at[level, f, way],
            recv_sem=recv_sem.at[level, f, way],
            device_id={"blk": beside(to)},
            device_id_type=MESH,
        )

    def first_copy(f, way):
        return copy(1, f, way, way, (sc, rc)[f].at[0, pl.ds((bx - RAD) * way, RAD)])

    for f, way in ((0, outer), (1, outer), (0, inner), (1, inner)):
        @pl.when(there(way))
        def _():
            first_copy(f, way).start()

    image_load = pltpu.make_async_copy(image_in.at[:, 0], image, out_sem.at[2])
    image_load.start()

    for side in (0, 1):
        @pl.when(jnp.logical_not(there(side)))
        def _():
            def clear(level, carry):
                for f in (0, 1):
                    wave[level, f, pl.ds((RAD + bx) * side, RAD)] = jnp.zeros(
                        (RAD, ny, nz), jnp.float32
                    )
                return carry

            lax.fori_loop(1, STEPS + 2, clear, 0)

    def arrive(level, f, side):
        @pl.when(there(side))
        def _():
            copy(level, f, 1 - side, side).wait_recv()

    def local(level, f):
        def group(g, carry):
            own = pl.ds(RAD * g, RAD)
            at = pl.ds(RAD + RAD * g, RAD)
            now = wave[level, f, at]
            high, low = split(now.reshape(rows, nz))
            both = dot(high, wz[...]) + dot(low, wz[...])
            side = dot(wy[...], high) + dot(wy[...], low)
            dz[f, at] = both[:, nz:].reshape(RAD, ny, nz)
            dzz = both[:, :nz].reshape(RAD, ny, nz) * (1.0 / SECOND_SCALE) + second_w[0] * now
            dyy = side.reshape(RAD, ny, nz) * (1.0 / SECOND_SCALE) + 2.0 * second_w[0] * now
            base[f, own] = (
                2.0 * now - wave[level - 1, f, at] + ch[own] * dyy + cv[own] * dzz
            )
            return carry

        lax.fori_loop(0, bx // RAD, group, 0)

    def rim(level, f, side):
        at = pl.ds((RAD + bx) * side, RAD)
        high, low = split(wave[level, f, at].reshape(rows, nz))
        weights = wz[:, nz:]
        dz[f, at] = (dot(high, weights) + dot(low, weights)).reshape(RAD, ny, nz)

    def update(level, f, side):
        half = ny // 2

        def plane(j, carry):
            own = (bx - RAD) * side + j
            x = own + RAD
            for r in (0, half):
                at = pl.ds(r, half)
                flat, cross = None, None
                for k in range(1, RAD + 1):
                    a = second_w[k] * (wave[level, f, x + k, at] + wave[level, f, x - k, at])
                    b = (first_w[k - 1] / FIRST_SCALE) * (dz[f, x + k, at] - dz[f, x - k, at])
                    flat = a if flat is None else flat + a
                    cross = b if cross is None else cross + b
                wave[level + 1, f, x, at] = (
                    base[f, own, at] + ch[own, at] * flat + cm[own, at] * cross
                )
            return carry

        lax.fori_loop(0, RAD, plane, 0, unroll=2)

    seconds = [(k, second_int[k]) for k in range(1, RAD + 1)]
    firsts = [(k + 1, first_int[k]) for k in range(RAD)]
    wz[:, :nz] = band(nz, seconds, False, nz)
    wz[:, nz:] = band(nz, firsts, True, nz)
    wy[...] = band(rows, seconds, False, ny)
    for load in loads:
        load.wait()
    for f in (0, 1):
        local(1, f)

    row_ids = lax.broadcasted_iota(jnp.int32, (ny, ny), 0)
    diagonal = row_ids == lax.broadcasted_iota(jnp.int32, (ny, ny), 1)
    depth_ids = lax.broadcasted_iota(jnp.int32, (ny, nz), 1).astype(jnp.float32)
    for x in range(bx):
        depths = live[0, pl.ds(x, 1), :].astype(jnp.float32)
        column = jnp.sum(jnp.where(diagonal, depths, 0.0), axis=1, keepdims=True)
        mute[x] = (depth_ids < column).astype(jnp.float32)
    mute_store = pltpu.make_async_copy(mute, mute_out, out_sem.at[3])
    mute_store.start()
    image_store = pltpu.make_async_copy(image, image_mid, out_sem.at[2])

    mid = [pltpu.make_async_copy(wave.at[3, f], snap.at[f], out_sem.at[f]) for f in (0, 1)]

    def slot_terms(slot, carry):
        shift = offsets[slot] - RAD

        def plane(x, inside):
            image[slot, x] += mute[x] * snap[0, RAD + x - shift] * snap[1, RAD + x + shift]
            return inside

        return lax.fori_loop(0, bx, plane, carry)

    def step(level, carry):
        for f in (0, 1):
            for side in (outer, inner):
                arrive(level, f, side)
                rim(level, f, side)
                update(level, f, side)

                @pl.when(there(side))
                def _():
                    copy(level + 1, f, side, side).start()

            @pl.when(level < STEPS)
            def _():
                local(level + 1, f)

            @pl.when(level == 3)
            def _():
                mid[f].start()
                if f == 1:
                    for item in mid + [image_load]:
                        item.wait()
                    lax.fori_loop(0, NOFF // 2, slot_terms, 0)

            if f == 0:
                @pl.when(level == STEPS)
                def _():
                    lax.fori_loop(NOFF // 2, NOFF, slot_terms, 0)
                    image_store.start()
        return carry

    lax.fori_loop(1, STEPS + 1, step, 0)

    last = STEPS + 1
    done = [mute_store, image_store]
    for f in (0, 1):
        own = pl.ds(RAD, bx)
        done.append(
            pltpu.make_async_copy(wave.at[last, f, own], snaps.at[f, own], last_sem.at[f, 2])
        )
        done[-1].start()

    for f in (0, 1):
        for j, side in enumerate((inner, outer)):
            arrive(last, f, side)
            at = pl.ds((RAD + bx) * side, RAD)
            done.append(
                pltpu.make_async_copy(wave.at[last, f, at], snaps.at[f, at], last_sem.at[f, j])
            )
            done[-1].start()
    for item in done:
        item.wait()
    for way in (0, 1):
        @pl.when(there(way))
        def _():
            for f in (0, 1):
                first_copy(f, way).wait_send()

            def sent(level, carry):
                for f in (0, 1):
                    copy(level, f, way, way).wait_send()
                return carry

            lax.fori_loop(2, STEPS + 2, sent, 0)


def image_kernel(
    offsets, snaps_in, mute_in, image_in, image_out, source_last, receiver_last,
    snaps, mute, image, load_sem, store_sem, side_sem,
):
    bx = mute.shape[0]
    sides = [
        pltpu.make_async_copy(snaps_in.at[0], snaps.at[0], side_sem.at[0]),
        pltpu.make_async_copy(snaps_in.at[1], snaps.at[1], side_sem.at[1]),
        pltpu.make_async_copy(mute_in, mute, side_sem.at[2]),
    ]
    for item in sides:
        item.start()

    def load(slot):
        return pltpu.make_async_copy(image_in.at[slot], image.at[slot], load_sem.at[slot])

    def store(slot):
        return pltpu.make_async_copy(image.at[slot], image_out.at[slot, 0], store_sem.at[slot])

    for slot in range(NOFF):
        load(slot).start()
    for item in sides:
        item.wait()
    lasts = [
        pltpu.make_async_copy(snaps.at[f, pl.ds(RAD, bx)], last.at[0], side_sem.at[3 + f])
        for f, last in enumerate((source_last, receiver_last))
    ]

    def terms(slot, carry):
        load(slot).wait()
        shift = offsets[slot] - RAD

        def plane(x, inside):
            image[slot, x] += mute[x] * snaps[0, RAD + x - shift] * snaps[1, RAD + x + shift]
            return inside

        lax.fori_loop(0, bx, plane, 0, unroll=True)
        store(slot).start()
        return carry

    lax.fori_loop(0, NOFF, terms, 0)
    for item in lasts:
        item.start()
    for slot in range(NOFF):
        store(slot).wait()
    for item in lasts:
        item.wait()


def per_device(
    count,
    source_prev,
    source_cur,
    receiver_prev,
    receiver_cur,
    coef_horiz,
    coef_vert,
    coef_mixed,
    live_depth,
    offsets,
    image_in,
):
    _, bx, ny, nz = source_cur.shape
    f32 = jnp.float32
    slab = pltpu.VMEM((bx, ny, nz), f32)
    full = bx + 2 * RAD
    hbm = pl.BlockSpec(memory_space=pltpu.HBM)
    any_space = pl.BlockSpec(memory_space=pl.ANY)
    snaps, image_mid, mute = pl.pallas_call(
        functools.partial(wave_kernel, count),
        out_shape=[
            jax.ShapeDtypeStruct((2, full, ny, nz), f32),
            jax.ShapeDtypeStruct((NOFF, bx, ny, nz), f32),
            jax.ShapeDtypeStruct((bx, ny, nz), f32),
        ],
        in_specs=[hbm] * 8
        + [pl.BlockSpec(memory_space=pltpu.VMEM), pl.BlockSpec(memory_space=pltpu.SMEM)],
        out_specs=[any_space] * 3,
        scratch_shapes=[
            pltpu.VMEM((STEPS + 2, 2, full, ny, nz), f32),
            pltpu.VMEM((2, full, ny, nz), f32),
            pltpu.VMEM((2, bx, ny, nz), f32),
            slab,
            slab,
            slab,
            pltpu.VMEM((nz, 2 * nz), jnp.bfloat16),
            pltpu.VMEM((RAD * ny, RAD * ny), jnp.bfloat16),
            pltpu.VMEM((NOFF, bx, ny, nz), f32),
            pltpu.VMEM((2, full, ny, nz), f32),
            slab,
            pltpu.SemaphoreType.DMA((7,)),
            pltpu.SemaphoreType.DMA((STEPS + 2, 2, 2)),
            pltpu.SemaphoreType.DMA((STEPS + 2, 2, 2)),
            pltpu.SemaphoreType.DMA((4,)),
            pltpu.SemaphoreType.DMA((2, 3)),
        ],
        compiler_params=pltpu.CompilerParams(
            collective_id=0, has_side_effects=True, vmem_limit_bytes=58 * 2**20
        ),
        name="wave_steps",
    )(
        source_prev, source_cur, receiver_prev, receiver_cur,
        coef_horiz, coef_vert, coef_mixed, image_in, live_depth, offsets,
    )
    return pl.pallas_call(
        image_kernel,
        in_specs=[pl.BlockSpec(memory_space=pltpu.SMEM)] + [hbm] * 3,
        out_specs=[hbm] * 3,
        scratch_shapes=[
            pltpu.VMEM((2, full, ny, nz), f32),
            slab,
            pltpu.VMEM((NOFF, bx, ny, nz), f32),
            pltpu.SemaphoreType.DMA((NOFF,)),
            pltpu.SemaphoreType.DMA((NOFF,)),
            pltpu.SemaphoreType.DMA((5,)),
        ],
        out_shape=[
            jax.ShapeDtypeStruct(image_in.shape, f32),
            jax.ShapeDtypeStruct(source_cur.shape, f32),
            jax.ShapeDtypeStruct(receiver_cur.shape, f32),
        ],
        compiler_params=pltpu.CompilerParams(vmem_limit_bytes=58 * 2**20),
        name="image_terms",
    )(offsets, snaps, mute, image_mid)


def solution(mesh):
    in_specs = (
        P(("shots", "blk"), None, None, None),
        P(("shots", "blk"), None, None, None),
        P(("shots", "blk"), None, None, None),
        P(("shots", "blk"), None, None, None),
        P("blk", None, None, None),
        P("blk", None, None, None),
        P("blk", None, None, None),
        P("blk", None, None),
        P(),
        P(None, ("shots", "blk"), None, None, None),
    )
    out_specs = (
        P(None, ("shots", "blk"), None, None, None),
        P(("shots", "blk"), None, None, None),
        P(("shots", "blk"), None, None, None),
    )
    return jax.shard_map(
        functools.partial(per_device, mesh.shape["blk"]),
        mesh=mesh,
        in_specs=in_specs,
        out_specs=out_specs,
        check_vma=False,
    )
```
